512 devices in a mesh: dp: 4 (over y_hi, core), expert: 32 (over y_lo, z), tensor: 4 (over x).
Axes of the slice: x: 4, y: 4 (y_hi: 2, y_lo: 2; y = y_hi * 2 + y_lo), z: 16, core: 2. Of those that a mesh axis runs over, the one named last changes fastest.
Arguments:
- grad_out: bfloat16 [16384, 7168], P(('dp', 'expert'), 'tensor'), may hold values from -2 to 2
- routes: int32 [16384, 2], P(('dp', 'expert')), may hold values from 0 to 31, all different within a row; in each aligned block of 128 rows (0 to 127, 128 to 255, ...) at most 12 rows name the same one
- probs: bfloat16 [16384, 2], P(('dp', 'expert')), may hold values from 0.099609375 to 1
- hidden: bfloat16 [32, 1536, 2432], P('expert', 'tensor', 'dp'), may hold values from -6 to 6
- weight: bfloat16 [32, 2432, 7168], P('expert', 'dp', 'tensor'), may hold values from -0.0625 to 0.0625
Outputs:
- grad_hidden: bfloat16 [32, 1536, 2432], P('expert', 'tensor', 'dp')
- grad_probs: float32 [16384, 2], P(('dp', 'expert'))
The draws below stay inside these ranges and needn't reach their ends.
Inputs may be any that keep to these rules, and one draw needn't show every extreme that they name: `routes`: among the 128 rows of one device's tokens no expert is named more than 12 times; the two experts of a token differ.
All inputs are finite; a program needn't handle non-finite values.
Results may differ from the reference program's by a relative error of at most 0.001.
Values may be sent and summed in bfloat16 or wider, within the bound.
A program may use at most 64 MiB of HBM per device.

```python
import math
import jax
import jax.numpy as jnp
import numpy as np
from jax import lax

D = 7168
FFX = 2432
TOK_GRP = 128
EXPERTS = 32
CAP = 12
SLOTS = 1536
TOKENS = 16384


def block_levels(own_key, shape, shards, smallest, largest):
    def one(position, blocks):
        steps = jax.random.uniform(jax.random.fold_in(jax.random.fold_in(own_key, 6), position), (blocks,), jnp.float32, smallest / len(shards), largest / len(shards))
        return jnp.repeat(jnp.exp(steps), shape[position] // blocks).reshape((-1,) + (1,) * (len(shape) - position - 1))

    factor_of = one(*shards[0])
    for cut in shards[1:]:
        factor_of = factor_of * one(*cut)
    return factor_of


def assign_block(stream_key, own, number, rows, number_of, top, most, skew):
    ranking = jax.random.permutation(stream_key, number_of)
    crowded, usual = portions_of(number_of, rows * top, most, skew, True), portions_of(number_of, rows * top, most, skew, False)
    places = jnp.arange(number_of)

    def named(tallies, offset_by):
        used = int((tallies > 0).sum())
        fixed = max(1, used // 4)
        shifted = fixed + (places - fixed + offset_by * (used - fixed)) % max(1, number_of - fixed)
        return jnp.zeros((number_of,), jnp.int32).at[ranking[jnp.where(places < fixed, places, shifted)]].set(jnp.asarray(tallies, jnp.int32))

    tallies = jnp.where(number % 4 == 0, named(crowded, number // 4), named(usual, number - number // 4 - 1))
    mixed = jax.random.permutation(jax.random.fold_in(own, 3), number_of)
    giver, sink = mixed[0:number_of // 2 * 2:2], mixed[1:number_of // 2 * 2:2]
    room = jnp.minimum(tallies[giver] - 1, most - tallies[sink]) // 2
    room = jnp.where((giver == ranking[0]) | (sink == ranking[0]) | (tallies[sink] == 0), 0, jnp.maximum(room, 0))
    shifted = jax.random.randint(jax.random.fold_in(own, 4), (number_of // 2,), 0, 1 << 20) % (room + 1)
    tallies = tallies.at[giver].add(-shifted).at[sink].add(shifted)
    members = jnp.searchsorted(jnp.cumsum(tallies), jnp.arange(rows * top), side="right").astype(jnp.int32)
    listing = members.reshape(top, rows).T
    listing = listing[jax.random.permutation(jax.random.fold_in(own, 1), rows)]
    offset_by = jax.random.randint(jax.random.fold_in(own, 2), (rows, 1), 0, top)
    return jnp.take_along_axis(listing, (jnp.arange(top)[None, :] + offset_by) % top, axis=1)


def portions_of(number_of, total, bound, skew, full):
    weights = [(1 << 20) // math.isqrt(grade ** skew) + 1 for grade in range(1, number_of + 1)]
    largest = bound if full else min(bound, max(-(-total // number_of), total * weights[0] // sum(weights)))
    least = 1 if total - largest >= number_of - 1 else 0
    given, spare = [largest] + [least] * (number_of - 1), total - largest - least * (number_of - 1)
    while spare > 0:
        candidates = [i for i in range(1, number_of) if given[i] < largest] or [i for i in range(1, number_of) if given[i] < bound]
        pool, remaining = sum([weights[i] for i in candidates]), spare
        for i in candidates:
            more = min(bound - given[i], max(1, remaining * weights[i] // pool), spare)
            given[i] = given[i] + more
            spare = spare - more
    return np.array(given)


def gaussian(key, shape, scale, reach, shards=(), kind=jnp.bfloat16):
    result = jax.random.normal(key, shape, jnp.float32) * scale
    if len(shards) > 0:
        result = block_levels(key, shape, shards, -0.22, 0.18) * result
    return jnp.clip(result, min=-reach, max=reach).astype(kind)


def setup_inputs(seed: int = 0) -> dict:
    key_list = jax.random.split(jax.random.key(seed), 6)
    grad_out = gaussian(key_list[0], (TOKENS, D), 0.3, 2.0, ((0, 128), (1, 4)))
    routes_keys = jax.random.split(jax.random.fold_in(key_list[1], 1), TOKENS // TOK_GRP)
    routes_turns = jax.random.permutation(jax.random.fold_in(key_list[1], 3), TOKENS // TOK_GRP)
    routes = jax.vmap(lambda own, number: assign_block(jax.random.fold_in(key_list[1], 2), own, number, TOK_GRP, EXPERTS, 2, CAP, 2))(routes_keys, routes_turns).reshape((TOKENS, 2))
    probs = jnp.clip(jnp.exp(math.log(1.0) - 2.306499 * jax.random.uniform(key_list[2], (TOKENS, 2), jnp.float32) ** block_levels(key_list[2], (TOKENS, 2), ((0, 128),), -0.2, 0.2)), 0.099609375, 1.0).astype(jnp.bfloat16)
    hidden = gaussian(key_list[3], (EXPERTS, SLOTS, FFX), 1.0, 6.0, ((0, 32), (1, 4), (2, 4)))
    weight = gaussian(key_list[4], (EXPERTS, FFX, D), D ** -0.5, 0.0625, ((0, 32), (1, 4), (2, 4)))
    return {"grad_out": grad_out, "routes": routes, "probs": probs, "hidden": hidden, "weight": weight}


def reference(grad_out, routes, probs, hidden, weight):
    tok_total = routes.shape[0]
    groups = tok_total // TOK_GRP
    onehot = (routes.reshape(groups, TOK_GRP * 2)[:, :, None] == jnp.arange(EXPERTS, dtype=jnp.int32)[None, None, :]).astype(jnp.int32)
    before = jnp.cumsum(onehot, axis=1) - onehot
    slot_index = jnp.sum(before * onehot, axis=2).reshape(tok_total, 2)
    source_group = (jnp.arange(tok_total, dtype=jnp.int32) // TOK_GRP)[:, None]
    slot_row = (source_group * CAP + slot_index).astype(jnp.int32)
    flat_row = slot_row.reshape(-1)
    flat_expert = routes.reshape(-1).astype(jnp.int32)
    flat_token = (jnp.arange(tok_total * 2, dtype=jnp.int32) // 2).astype(jnp.int32)
    token_rows = grad_out[flat_token]
    flat_prob = probs.reshape(-1)

    def per_expert(expert_id):
        target = jnp.where(flat_expert == expert_id, flat_row, SLOTS).astype(jnp.int32)
        dout_slots = jnp.zeros((SLOTS, D), jnp.bfloat16).at[target].set(token_rows, mode="drop")
        prob_slots = jnp.zeros((SLOTS,), jnp.bfloat16).at[target].set(flat_prob, mode="drop")
        back = jnp.dot(dout_slots, weight[expert_id].T, preferred_element_type=jnp.float32)
        grad_h = (prob_slots.astype(jnp.float32)[:, None] * back).astype(jnp.bfloat16)
        score = jnp.sum(hidden[expert_id].astype(jnp.float32) * back, axis=1)
        return grad_h, score

    grad_hidden, score = lax.map(per_expert, jnp.arange(EXPERTS, dtype=jnp.int32))
    grad_probs = score[flat_expert, flat_row].reshape(tok_total, 2)
    return grad_hidden, grad_probs
```

```python
import jax
import jax.numpy as jnp
from jax import lax
from jax.experimental import pallas as pl
from jax.experimental.pallas import tpu as pltpu
from jax.sharding import PartitionSpec as P

MESH = pl.DeviceIdType.MESH
F32 = jnp.float32
BF16 = jnp.bfloat16

TOK = 128
CAP = 12
Z = 16
PAIRS = Z // 2
EXP = 2 * Z
D = 1792
HALF = D // 2
MSG = D + HALF
FFX = 608
FP = 640
SLOTS = 384
UNITS = 2 * PAIRS


def iota(shape, dim):
    return lax.broadcasted_iota(jnp.int32, shape, dim)


def dot(a, b, **kw):
    return jnp.dot(a, b, preferred_element_type=F32, **kw)


def dot_t(a, b):
    return lax.dot_general(a, b, (((1,), (1,)), ((), ())), preferred_element_type=F32)


def offset(k):
    half = lax.shift_right_logical(k + 1, 1)
    return jnp.where(lax.rem(k, 2) == 1, half, -half)


def kernel(
    grad_hbm, routes_ref, probs_ref, hidden_hbm, weight_hbm,
    gh_hbm, gp_ref,
    tokens, sel, send, recv, w_buf, h_buf, part, relay, fin, out_buf,
    prob_out, prob_in, prob_col, score, score_sum, score_in, table, hot, pick,
    local_sem, ex_send, ex_recv, z_send, z_recv, y_send, sib_send, x_recv,
    p_send, p_recv, xs_send, relay_recv, fin_recv, dp_send, dp_recv, s_send, s_recv,
):
    dp = lax.axis_index("dp")
    ex = lax.axis_index("expert")
    x = lax.axis_index("tensor")
    h, c = lax.div(dp, 2), lax.rem(dp, 2)
    l, z = lax.div(ex, Z), lax.rem(ex, Z)
    y = 2 * h + l
    pair = lax.div(z, 2)
    direct = c == l
    zi = jnp.where(direct, y, 4)
    sibling = (2 * h + 1 - c, ex, x)

    load_grad = pltpu.make_async_copy(grad_hbm, tokens.at[0], local_sem.at[0])
    load_w = pltpu.make_async_copy(weight_hbm.at[0], w_buf.at[pl.ds(0, FFX)], local_sem.at[1])
    load_h = pltpu.make_async_copy(hidden_hbm.at[0], h_buf, local_sem.at[2])
    load_grad.start()
    load_w.start()
    load_h.start()

    barrier = pltpu.get_barrier_semaphore()

    def greet(device):
        pl.semaphore_signal(barrier, inc=1, device_id=device, device_id_type=MESH)

    def greet_z(i, carry):
        greet((dp, l * Z + lax.rem(z + i, Z), x))
        return carry

    lax.fori_loop(1, Z, greet_z, 0)
    greet(sibling)
    greet((2 * (1 - h) + c, ex, x))
    greet((2 * (1 - h) + 1 - c, ex, x))
    greet((c, (1 - l) * Z + z, x))
    greet((2 + c, (1 - l) * Z + z, x))
    for i in range(1, 4):
        greet((dp, ex, lax.rem(x + i, 4)))
    twin = x == dp

    def greet_t(i, carry):
        @pl.when(jnp.logical_or(jnp.logical_not(twin), i != ex))
        def _():
            greet((x, i, dp))

        return carry

    lax.fori_loop(0, EXP, greet_t, 0)

    lane, sub = iota((TOK, TOK), 1), iota((TOK, TOK), 0)
    hot0 = (routes_ref[:, 0:1] == lane).astype(F32)
    hot1 = (routes_ref[:, 1:2] == lane).astype(F32)
    both = hot0 + hot1
    earlier = dot((sub > lane).astype(BF16), both.astype(BF16))
    number = jnp.where(both > 0, earlier + 1.0, 0.0)
    number_t = jnp.transpose(number).astype(BF16)

    def selection(lam):
        row, col = iota((SLOTS, TOK), 0), iota((SLOTS, TOK), 1)
        first = row < 16 * Z
        rest = row - 16 * Z
        zz = jnp.where(first, row >> 4, rest >> 3)
        g = jnp.where(first, (row >> 3) & 1, (rest >> 2) & 1)
        s = jnp.where(first, row & 7, 8 + (rest & 3))
        expand = jnp.logical_and(col == lam * Z + zz, g == c).astype(BF16)
        return (dot(expand, number_t) == (s + 1).astype(F32)).astype(BF16)

    sel[2] = selection(1 - c)
    sel[0] = selection(c)
    probs = probs_ref[...].astype(F32)
    prob_table = jnp.zeros((TOK, TOK), F32)
    for k, hk in enumerate((hot0, hot1)):
        slot = jnp.sum(hk * earlier, axis=1, keepdims=True)
        prob_table += dot(
            jnp.transpose(hk * probs[:, k : k + 1]).astype(BF16),
            (slot == lane.astype(F32)).astype(BF16),
        )
        hot[k] = hk
        pick[k] = (slot.astype(jnp.int32) + lax.rem(z, 4) * CAP == lane).astype(F32)
    for e in range(EXP):
        prob_out[e] = prob_table[e : e + 1, :]

    load_grad.wait()
    pl.semaphore_wait(barrier, jnp.where(twin, 54, 55))

    send_sel = pltpu.make_async_remote_copy(
        sel.at[2], sel.at[1], ex_send.at[0], ex_recv.at[0], device_id=sibling, device_id_type=MESH
    )
    send_tokens = pltpu.make_async_remote_copy(
        tokens.at[0], tokens.at[1], ex_send.at[1], ex_recv.at[1], device_id=sibling, device_id_type=MESH
    )
    send_sel.start()
    send_tokens.start()

    def scatter(source, index, target, sent, got):
        def one(n, carry):
            own = jnp.logical_and(twin, n == ex)

            @pl.when(own)
            def _():
                pltpu.make_async_copy(source.at[index(n)], target.at[ex], got).start()

            @pl.when(jnp.logical_not(own))
            def _():
                pltpu.make_async_remote_copy(
                    source.at[index(n)], target.at[ex], sent, got, device_id=(x, n, dp), device_id_type=MESH
                ).start()

            return carry

        lax.fori_loop(0, EXP, one, 0)

    def scatter_sent(target, sent):
        @pl.when(twin)
        def _():
            ref = target.at[pl.ds(0, EXP - 1)]
            pltpu.make_async_copy(ref, ref, sent).wait()

        @pl.when(jnp.logical_not(twin))
        def _():
            pltpu.make_async_copy(target, target, sent).wait()

    scatter(prob_out, lambda n: n, prob_in, p_send, p_recv)

    send_sel.wait_recv()
    send_tokens.wait_recv()
    for n in range(0, D, 256):
        block = dot(sel[0, 0 : 16 * Z], tokens[0, :, n : n + 256])
        block += dot(sel[1, 0 : 16 * Z], tokens[1, :, n : n + 256])
        send[:, :, n : n + 256] = block.reshape(Z, 16, 256).astype(BF16)
    for n in range(0, HALF, 128):
        halves = []
        for at in (n, HALF + n):
            block = dot(sel[0, 16 * Z :], tokens[0, :, at : at + 128])
            block += dot(sel[1, 16 * Z :], tokens[1, :, at : at + 128])
            halves.append(block.reshape(Z, 8, 128))
        send[:, :, D + n : D + n + 128] = jnp.concatenate(halves, axis=1).astype(BF16)

    def send_z(i, carry):
        to = 2 * lax.rem(pair + offset(lax.div(i, 2)) + PAIRS, PAIRS) + lax.rem(i, 2)

        @pl.when(to == z)
        def _():
            pltpu.make_async_copy(send.at[to], recv.at[zi, z], z_recv.at[z]).start()

        @pl.when(to != z)
        def _():
            pltpu.make_async_remote_copy(
                send.at[to], recv.at[zi, z], z_send, z_recv.at[z],
                device_id=(dp, l * Z + to, x), device_id_type=MESH,
            ).start()

        return carry

    lax.fori_loop(0, Z, send_z, 0)

    pltpu.make_async_copy(prob_in, prob_in, p_recv).wait()
    for e in range(EXP):
        table[e : e + 1, :] = prob_in[e]
    row, col = iota((SLOTS, EXP), 0), iota((SLOTS, EXP), 1)
    spread = dot(((row * 5462) >> 16 == col).astype(BF16), table[...].astype(BF16))
    row, col = iota((SLOTS, TOK), 0), iota((SLOTS, TOK), 1)
    mine = row - CAP * ((row * 5462) >> 16) == col
    prob_col[...] = jnp.broadcast_to(jnp.sum(jnp.where(mine, spread, 0.0), axis=1, keepdims=True), (SLOTS, TOK))
    w_buf[FFX:FP, :] = jnp.zeros((FP - FFX, D), BF16)
    load_w.wait()
    load_h.wait()

    def place(ys, rp):
        return recv.at[ys, pl.ds(2 * rp, 2)]

    def arrived(ys, rp):
        pltpu.make_async_copy(place(ys, rp), place(ys, rp), x_recv.at[ys, rp]).wait()

    def to_sibling(ys, rp):
        pltpu.make_async_remote_copy(
            place(ys, rp), place(ys, rp), sib_send.at[ys], x_recv.at[ys, rp],
            device_id=sibling, device_id_type=MESH,
        ).start()

    def along_y(i, rp, device):
        pltpu.make_async_remote_copy(
            place(zi, rp), place(y, rp), y_send.at[i], x_recv.at[y, rp], device_id=device, device_id_type=MESH
        ).start()

    def origin(k):
        return lax.rem(pair - offset(k) + PAIRS, PAIRS)

    def stage_z(k):
        rp = origin(k)
        for i in range(2):
            ref = recv.at[zi, 2 * rp + i]
            pltpu.make_async_copy(ref, ref, z_recv.at[2 * rp + i]).wait()

        @pl.when(direct)
        def _():
            along_y(0, rp, (2 * (1 - h) + c, ex, x))
            to_sibling(y, rp)

        @pl.when(jnp.logical_not(direct))
        def _():
            along_y(0, rp, (c, (1 - l) * Z + z, x))
            along_y(1, rp, (2 + c, (1 - l) * Z + z, x))

    def stage_y(k):
        rp = origin(k)

        @pl.when(direct)
        def _():
            for i in (1, 3, 2):
                ys = lax.rem(y + i, 4)
                arrived(ys, rp)
                to_sibling(ys, rp)

        @pl.when(jnp.logical_not(direct))
        def _():
            for ys in range(4):
                arrived(ys, rp)

    def along_x(i, source, target, got, device_x):
        pltpu.make_async_remote_copy(
            source, target, xs_send.at[i], got, device_id=(dp, ex, device_x), device_id_type=MESH
        ).start()

    def turn(lo):
        return 1 if lo == 0 else 3

    def compute(k):
        rp = origin(k)
        rows = [(lo, hi) for lo in range(2) for hi in range(2)]
        whole = [recv[2 * hi + lo, pl.ds(2 * rp, 2), :, 0:D].reshape(32, D) for lo, hi in rows]
        folded = [recv[2 * hi + lo, pl.ds(2 * rp, 2), :, D:MSG].reshape(32, HALF) for lo, hi in rows]
        first = jnp.concatenate([v[:, :HALF] for v in whole] + folded, axis=0)
        second = jnp.concatenate([v[:, HALF:] for v in whole] + folded, axis=0)
        for n0, n1 in ((0, 256), (256, 512), (512, 640)):
            left = dot_t(first, w_buf[n0:n1, :HALF])
            right = dot_t(second, w_buf[n0:n1, HALF:])
            low = iota((8, n1 - n0), 0) < 4
            for b, (lo, hi) in enumerate(rows):
                u = 2 * rp + lo
                ends = []
                for zz in range(2):
                    at = 32 * b + 16 * zz
                    for g in range(2):
                        v = left[at + 8 * g : at + 8 * g + 8] + right[at + 8 * g : at + 8 * g + 8]
                        part[u, 2 * hi + g, 8 * zz : 8 * zz + 8, n0:n1] = v
                    at += 128
                    ends.append(left[at : at + 8] + right[at + 8 : at + 16])
                part[u, 2 * hi, 16:24, n0:n1] = jnp.where(low, ends[0], pltpu.roll(ends[1], 4, 0))
                part[u, 2 * hi + 1, 16:24, n0:n1] = jnp.where(low, pltpu.roll(ends[0], 4, 0), ends[1])
        for lo in range(2):
            u, s = 2 * rp + lo, turn(lo)
            along_x(0, part.at[u, lax.rem(x + 2, 4)], relay.at[u], relay_recv.at[u], lax.rem(x + s, 4))
            back_x = lax.rem(x + 4 - s, 4)
            along_x(1, part.at[u, back_x], fin.at[1, u], fin_recv.at[1, u], back_x)

    def add_x(k):
        rp = origin(k)
        for lo in range(2):
            u = 2 * rp + lo
            to = lax.rem(x + turn(lo), 4)
            pltpu.make_async_copy(relay.at[u], relay.at[u], relay_recv.at[u]).wait()
            part[u, to] = part[u, to] + relay[u]
            along_x(2, part.at[u, to], fin.at[0, u], fin_recv.at[0, u], to)

    def step(k, carry):
        @pl.when(k < PAIRS)
        def _():
            stage_z(k)

        @pl.when(k >= 2)
        def _():
            add_x(k - 2)

        @pl.when(k >= 1)
        def _():
            stage_y(k - 1)
            compute(k - 1)

        return carry

    lax.fori_loop(0, PAIRS + 1, step, 0)
    add_x(PAIRS - 1)

    def wait_fin(u, carry):
        for i in range(2):
            pltpu.make_async_copy(fin.at[i, u], fin.at[i, u], fin_recv.at[i, u]).wait()
        return carry

    lax.fori_loop(0, UNITS, wait_fin, 0)

    def finish(q, carry):
        lo, j = lax.div(q, 4), lax.rem(q, 4)
        low = iota((8, FP), 0) < 4
        tiles = []
        for i in range(2):
            u = 2 * (2 * j + i) + lo
            total = part[u, x] + (fin[0, u] + fin[1, u])
            middle, end = pltpu.roll(total[8:16], 4, 0), total[16:24]
            tiles += [total[0:8], jnp.where(low, end, middle), jnp.where(low, middle, end)]
        back = jnp.concatenate(tiles, axis=0)[:, :FFX]
        rows = pl.ds(pl.multiple_of(48 * q, 16), 48)
        out_buf[rows, :] = (prob_col[rows, 0:1] * back).astype(BF16)
        col = jnp.sum(h_buf[rows, :].astype(F32) * back, axis=1, keepdims=True)
        score[dp, q] = jnp.sum(jnp.where(iota((48, TOK), 0) == iota((48, TOK), 1), col, 0.0), axis=0, keepdims=True)
        return carry

    lax.fori_loop(0, 8, finish, 0)
    store = pltpu.make_async_copy(out_buf, gh_hbm.at[0], local_sem.at[3])
    store.start()
    for i in range(1, 4):
        pltpu.make_async_remote_copy(
            score.at[dp], score.at[dp], dp_send, dp_recv,
            device_id=(lax.rem(dp + i, 4), ex, x), device_id_type=MESH,
        ).start()
    three = score.at[pl.ds(0, 3)]
    pltpu.make_async_copy(three, three, dp_recv).wait()
    score_sum[...] = (score[0] + score[1]) + (score[2] + score[3])
    scatter(score_sum, lambda n: lax.div(n, 4), score_in, s_send, s_recv)
    pltpu.make_async_copy(score_in, score_in, s_recv).wait()
    for e in range(EXP):
        table[e : e + 1, :] = score_in[e]
    for k in range(2):
        rows = dot(hot[k, :, 0:EXP], table[...], precision=lax.Precision.HIGHEST)
        gp_ref[:, k : k + 1] = jnp.sum(rows * pick[k], axis=1, keepdims=True)

    send_sel.wait_send()
    send_tokens.wait_send()
    scatter_sent(prob_in, p_send)
    scatter_sent(score_in, s_send)
    sent = send.at[pl.ds(0, Z - 1)]
    pltpu.make_async_copy(sent, sent, z_send).wait()
    pltpu.make_async_copy(send, send, y_send.at[0]).wait()

    @pl.when(direct)
    def _():
        for ys in range(4):
            pltpu.make_async_copy(send, send, sib_send.at[ys]).wait()

    @pl.when(jnp.logical_not(direct))
    def _():
        pltpu.make_async_copy(send, send, y_send.at[1]).wait()

    for i in range(3):
        pltpu.make_async_copy(relay, relay, xs_send.at[i]).wait()
    pltpu.make_async_copy(three, three, dp_send).wait()
    store.wait()


def shards(grad_out, routes, probs, hidden, weight):
    dma = pltpu.SemaphoreType.DMA
    vmem, hbm = pl.BlockSpec(memory_space=pltpu.VMEM), pl.BlockSpec(memory_space=pl.ANY)
    return pl.pallas_call(
        kernel,
        out_shape=(
            jax.ShapeDtypeStruct((1, SLOTS, FFX), BF16),
            jax.ShapeDtypeStruct((TOK, 2), F32),
        ),
        in_specs=[hbm, vmem, vmem, hbm, hbm],
        out_specs=(hbm, vmem),
        scratch_shapes=[
            pltpu.VMEM((2, TOK, D), BF16),
            pltpu.VMEM((3, SLOTS, TOK), BF16),
            pltpu.VMEM((Z, 16, MSG), BF16),
            pltpu.VMEM((5, Z, 16, MSG), BF16),
            pltpu.VMEM((FP, D), BF16),
            pltpu.VMEM((SLOTS, FFX), BF16),
            pltpu.VMEM((UNITS, 4, 24, FP), F32),
            pltpu.VMEM((UNITS, 24, FP), F32),
            pltpu.VMEM((2, UNITS, 24, FP), F32),
            pltpu.VMEM((SLOTS, FFX), BF16),
            pltpu.VMEM((EXP, 1, TOK), F32),
            pltpu.VMEM((EXP, 1, TOK), F32),
            pltpu.VMEM((SLOTS, TOK), F32),
            pltpu.VMEM((4, 8, 1, TOK), F32),
            pltpu.VMEM((8, 1, TOK), F32),
            pltpu.VMEM((EXP, 1, TOK), F32),
            pltpu.VMEM((EXP, TOK), F32),
            pltpu.VMEM((2, TOK, TOK), F32),
            pltpu.VMEM((2, TOK, TOK), F32),
            dma((4,)),
            dma((2,)),
            dma((2,)),
            dma,
            dma((Z,)),
            dma((2,)),
            dma((4,)),
            dma((4, PAIRS)),
            dma,
            dma,
            dma((3,)),
            dma((UNITS,)),
            dma((2, UNITS)),
            dma,
            dma,
            dma,
            dma,
        ],
        compiler_params=pltpu.CompilerParams(
            collective_id=0, has_side_effects=True, vmem_limit_bytes=48 * 1024 * 1024
        ),
        name="moe_down_backward",
    )(grad_out, routes, probs, hidden, weight)


def solution(mesh):
    return jax.shard_map(
        shards,
        mesh=mesh,
        in_specs=(
            P(("dp", "expert"), "tensor"),
            P(("dp", "expert"), None),
            P(("dp", "expert"), None),
            P("expert", "tensor", "dp"),
            P("expert", "dp", "tensor"),
        ),
        out_specs=(P("expert", "tensor", "dp"), P(("dp", "expert"), None)),
        check_vma=False,
    )
```

```python
import jax
import jax.numpy as jnp
from jax import lax
from jax.experimental import pallas as pl
from jax.experimental.pallas import tpu as pltpu
from jax.sharding import PartitionSpec as P

ORDER = (0, 1, -1, 2, -2, 3, -3, 4)
AHEAD = 3
SEQ = "ZYCAFG"
LAGS = dict(Z=0, Y=1, C=1, A=2, F=3, G=4)
MESH = pl.DeviceIdType.MESH
F32 = jnp.float32
BF16 = jnp.bfloat16

TOK = 128
CAP = 12
Z = 16
PAIRS = Z // 2
EXP = 2 * Z
D = 1792
HALF = D // 2
MSG = D + HALF
FFX = 608
FP = 640
SLOTS = 384
UNITS = 2 * PAIRS


def iota(shape, dim):
    return lax.broadcasted_iota(jnp.int32, shape, dim)


def dot(a, b, **kw):
    return jnp.dot(a, b, preferred_element_type=F32, **kw)


def dot_t(a, b):
    return lax.dot_general(a, b, (((1,), (1,)), ((), ())), preferred_element_type=F32)


def offset(k):
    at = ORDER[0]
    for i, o in enumerate(ORDER[1:], 1):
        at = jnp.where(k == i, o, at)
    return at


def turn(lo):
    return 1 if lo == 0 else 3


def kernel(
    grad_hbm, routes_ref, probs_ref, hidden_hbm, weight_hbm,
    gh_hbm, gp_ref,
    tokens, send, zbuf, other, recv, w_buf, h_buf, hidden, part, relay, fin, result, out_buf,
    prob_out, prob_in, prob_col, score, score_sum, score_in, table, hot, slots,
    local_sem, z_send, z_recv, y_send, sib_send, x_recv,
    p_send, p_recv, xs_send, relay_recv, fin_recv, dp_send, dp_recv, s_send, s_recv,
):
    dp = lax.axis_index("dp")
    ex = lax.axis_index("expert")
    x = lax.axis_index("tensor")
    h, c = lax.div(dp, 2), lax.rem(dp, 2)
    l, z = lax.div(ex, Z), lax.rem(ex, Z)
    y = 2 * h + l
    pair = lax.div(z, 2)
    sibling = (2 * h + 1 - c, ex, x)
    opposite = (2 * (1 - h) + c, ex, x)
    beside = ((c, (1 - l) * Z + z, x), (2 + c, (1 - l) * Z + z, x))

    load_grad = pltpu.make_async_copy(grad_hbm, tokens, local_sem.at[0])
    load_w = pltpu.make_async_copy(weight_hbm.at[0], w_buf.at[pl.ds(0, FFX)], local_sem.at[1])
    load_h = pltpu.make_async_copy(hidden_hbm.at[0], h_buf.at[pl.ds(0, FFX)], local_sem.at[2])
    load_grad.start()
    load_w.start()
    load_h.start()

    barrier = pltpu.get_barrier_semaphore()

    def greet(device):
        pl.semaphore_signal(barrier, inc=1, device_id=device, device_id_type=MESH)

    def greet_z(i, carry):
        greet((dp, l * Z + lax.rem(z + i, Z), x))
        return carry

    lax.fori_loop(1, Z, greet_z, 0)
    greet(sibling)
    greet(opposite)
    greet((2 * (1 - h) + 1 - c, ex, x))
    greet(beside[0])
    greet(beside[1])
    for i in range(1, 4):
        greet((dp, ex, lax.rem(x + i, 4)))
    twin = x == dp

    def greet_t(i, carry):
        @pl.when(jnp.logical_or(jnp.logical_not(twin), i != ex))
        def _():
            greet((x, i, dp))

        return carry

    lax.fori_loop(0, EXP, greet_t, 0)

    expert = iota((EXP, TOK), 0)
    hots = [(routes_ref[k : k + 1, :] == expert).astype(F32) for k in range(2)]
    both = hots[0] + hots[1]
    before = (iota((TOK, TOK), 0) < iota((TOK, TOK), 1)).astype(BF16)
    earlier = dot(both.astype(BF16), before)
    number = jnp.where(both > 0, earlier + 1.0, 0.0).astype(BF16)
    row, col = iota((SLOTS, EXP), 0), iota((SLOTS, EXP), 1)
    first, rest = row < 16 * Z, row - 16 * Z
    zz = jnp.where(first, row >> 4, rest >> 3)
    lam = jnp.where(first, (row >> 3) & 1, (rest >> 2) & 1)
    spread = dot((col == lam * Z + zz).astype(BF16), number)
    row = iota((SLOTS, TOK), 0)
    slot = jnp.where(row < 16 * Z, row & 7, 8 + (row & 3))
    select = (spread == (slot + 1).astype(F32)).astype(BF16)

    load_grad.wait()
    for n in range(0, D, 256):
        block = dot(select[0 : 16 * Z], tokens[:, n : n + 256])
        send[:, :, n : n + 256] = block.reshape(Z, 16, 256).astype(BF16)
    for n in range(0, HALF, 128):
        halves = []
        for at in (n, HALF + n):
            block = dot(select[16 * Z :], tokens[:, at : at + 128])
            halves.append(block.reshape(Z, 8, 128))
        send[:, :, D + n : D + n + 128] = jnp.concatenate(halves, axis=1).astype(BF16)

    pl.semaphore_wait(barrier, jnp.where(twin, 54, 55))

    def send_z(k):
        for i in range(2):
            to = 2 * lax.rem(pair + offset(k) + PAIRS, PAIRS) + i

            @pl.when(to == z)
            def _():
                pltpu.make_async_copy(send.at[to], zbuf.at[z], z_recv.at[z]).start()

            @pl.when(to != z)
            def _():
                pltpu.make_async_remote_copy(
                    send.at[to], zbuf.at[z], z_send, z_recv.at[z],
                    device_id=(dp, l * Z + to, x), device_id_type=MESH,
                ).start()

    def send_first(k, carry):
        send_z(k)
        return carry

    lax.fori_loop(0, AHEAD, send_first, 0)

    def small(source, target, n, sent, got):
        own = jnp.logical_and(twin, n == ex)

        @pl.when(own)
        def _():
            pltpu.make_async_copy(source, target, got).start()

        @pl.when(jnp.logical_not(own))
        def _():
            pltpu.make_async_remote_copy(
                source, target, sent, got, device_id=(x, n, dp), device_id_type=MESH
            ).start()

    def small_sent(target, sent):
        @pl.when(twin)
        def _():
            ref = target.at[pl.ds(0, EXP - 1)]
            pltpu.make_async_copy(ref, ref, sent).wait()

        @pl.when(jnp.logical_not(twin))
        def _():
            pltpu.make_async_copy(target, target, sent).wait()

    probs = probs_ref[...].astype(F32)
    weights = jnp.zeros((EXP, TOK), F32)
    for k in range(2):
        at = jnp.sum(hots[k] * earlier, axis=0, keepdims=True).astype(jnp.int32)
        weights += dot_t(
            (hots[k] * probs[k : k + 1, :]).astype(BF16), (iota((TOK, TOK), 0) == at).astype(BF16)
        )
        hot[k] = hots[k]
        slots[k] = jnp.broadcast_to(at + lax.rem(z, 2) * CAP, (8, TOK))
    for e in range(EXP):
        prob_out[e] = weights[e : e + 1, :]

    def send_prob(n, carry):
        small(prob_out.at[n], prob_in.at[ex], n, p_send, p_recv)
        return carry

    lax.fori_loop(0, EXP, send_prob, 0)

    h_buf[FFX:FP, :] = jnp.zeros((FP - FFX, SLOTS), BF16)
    w_buf[FFX:FP, :] = jnp.zeros((FP - FFX, D), BF16)
    table[...] = jnp.zeros((TOK, TOK), F32)
    load_h.wait()
    for i in range(0, SLOTS, 128):
        for j in range(0, FP, 128):
            hidden[i : i + 128, j : j + 128] = jnp.transpose(h_buf[j : j + 128, i : i + 128].astype(F32))
    load_w.wait()

    def take_prob():
        pltpu.make_async_copy(prob_in, prob_in, p_recv).wait()
        for e in range(EXP):
            table[e : e + 1, :] = prob_in[e]
        row, col = iota((SLOTS, EXP), 0), iota((SLOTS, EXP), 1)
        spread = dot(((row * 5462) >> 16 == col).astype(BF16), table[0:EXP].astype(BF16))
        row, col = iota((SLOTS, TOK), 0), iota((SLOTS, TOK), 1)
        mine = row - CAP * ((row * 5462) >> 16) == col
        prob_col[...] = jnp.broadcast_to(jnp.sum(jnp.where(mine, spread, 0.0), axis=1, keepdims=True), (SLOTS, TOK))

    def origin(k):
        return lax.rem(pair - offset(k) + PAIRS, PAIRS)

    def forward(source, core, ys, rp, sent, device):
        pltpu.make_async_remote_copy(
            source, recv.at[core, ys, rp], sent, x_recv.at[core, ys, rp], device_id=device, device_id_type=MESH
        ).start()

    def arrived(core, ys, rp):
        ref = recv.at[core, ys, rp]
        pltpu.make_async_copy(ref, ref, x_recv.at[core, ys, rp]).wait()

    def stage_z(k):
        rp = origin(k)
        for i in range(2):
            ref = zbuf.at[2 * rp + i]
            pltpu.make_async_copy(ref, ref, z_recv.at[2 * rp + i]).wait()
        both = zbuf[pl.ds(2 * rp, 2)].reshape(32, MSG)
        row, col = iota((32, 32), 0), iota((32, 32), 1)
        v = jnp.where(row < 16, l, 1 - l)
        eight, four = row & 7, row & 3
        whole = dot((col == 16 * ((row >> 3) & 1) + 8 * v + eight).astype(BF16), both[:, :D]).astype(BF16)
        at = 16 * ((eight >> 2) & 1) + 8 * ((row >> 3) & 1) + 4 * v + four
        folded = dot((col == at).astype(BF16), both[:, D:]).astype(BF16)
        recv[c, y, rp, :, 0:D] = whole[0:16]
        recv[c, y, rp, :, D:MSG] = folded[0:16]
        other[rp, :, 0:D] = whole[16:32]
        other[rp, :, D:MSG] = folded[16:32]
        forward(other.at[rp], c, y, rp, y_send.at[0], beside[0])
        forward(other.at[rp], c, y, rp, y_send.at[1], beside[1])
        forward(recv.at[c, y, rp], c, y, rp, y_send.at[2], opposite)
        forward(recv.at[c, y, rp], c, y, rp, sib_send.at[y], sibling)

    def stage_y(k):
        rp = origin(k)
        for i in (1, 3, 2):
            ys = lax.rem(y + i, 4)
            arrived(c, ys, rp)
            forward(recv.at[c, ys, rp], c, ys, rp, sib_send.at[ys], sibling)

    def along_x(i, source, target, got, device_x):
        pltpu.make_async_remote_copy(
            source, target, xs_send.at[i], got, device_id=(dp, ex, device_x), device_id_type=MESH
        ).start()

    def compute(k):
        rp = origin(k)
        for ys in range(4):
            arrived(1 - c, ys, rp)
        rows = [(lo, hi, core) for lo in range(2) for hi in range(2) for core in range(2)]
        whole = [recv[core, 2 * hi + lo, rp, :, 0:D] for lo, hi, core in rows]
        folded = [recv[core, 2 * hi + lo, rp, :, D:MSG] for lo, hi, core in rows]
        left_rows = jnp.concatenate([v[:, :HALF] for v in whole] + folded, axis=0)
        right_rows = jnp.concatenate([v[:, HALF:] for v in whole] + folded, axis=0)
        for n0, n1 in ((0, 256), (256, 512), (512, 640)):
            left = dot_t(left_rows, w_buf[n0:n1, :HALF])
            right = dot_t(right_rows, w_buf[n0:n1, HALF:])
            for i, (lo, hi, core) in enumerate(rows):
                at = 16 * i
                part[2 * rp + lo, 2 * hi + core, 0:16, n0:n1] = left[at : at + 16] + right[at : at + 16]
                at += 128
                part[2 * rp + lo, 2 * hi + core, 16:24, n0:n1] = left[at : at + 8] + right[at + 8 : at + 16]
        for lo in range(2):
            u, s = 2 * rp + lo, turn(lo)
            along_x(0, part.at[u, lax.rem(x + 2, 4)], relay.at[u], relay_recv.at[u], lax.rem(x + s, 4))
            back_x = lax.rem(x + 4 - s, 4)
            along_x(1, part.at[u, back_x], fin.at[1, u], fin_recv.at[1, u], back_x)

    def add_x(k):
        rp = origin(k)
        for lo in range(2):
            u = 2 * rp + lo
            to = lax.rem(x + turn(lo), 4)
            pltpu.make_async_copy(relay.at[u], relay.at[u], relay_recv.at[u]).wait()
            part[u, to] = part[u, to] + relay[u]
            along_x(2, part.at[u, to], fin.at[0, u], fin_recv.at[0, u], to)

    def finish(k):
        rp = origin(k)
        for lo in range(2):
            u = 2 * rp + lo
            for i in range(2):
                pltpu.make_async_copy(fin.at[i, u], fin.at[i, u], fin_recv.at[i, u]).wait()
            total = part[u, x] + (fin[0, u] + fin[1, u])
            low = iota((8, FP), 0) < 4
            middle, end = pltpu.roll(total[8:16], 4, 0), total[16:24]
            total = jnp.concatenate(
                [total[0:8], jnp.where(low, end, middle), jnp.where(low, middle, end)], axis=0
            )
            rows = pl.ds(pl.multiple_of(192 * lo + 24 * rp, 8), 24)
            result[rows, :] = prob_col[rows, 0:1] * total
            col = jnp.sum(hidden[rows, :] * total, axis=1, keepdims=True)
            score[dp, u] = jnp.sum(
                jnp.where(iota((24, TOK), 0) == iota((24, TOK), 1), col, 0.0), axis=0, keepdims=True
            )
        ref = score.at[dp, pl.ds(2 * rp, 2)]
        for i in range(1, 4):
            pltpu.make_async_remote_copy(
                ref, ref, dp_send, dp_recv.at[rp], device_id=(lax.rem(dp + i, 4), ex, x), device_id_type=MESH
            ).start()

    def give(k):
        rp = origin(k)
        three = score.at[0, pl.ds(0, 6)]
        pltpu.make_async_copy(three, three, dp_recv.at[rp]).wait()
        for lo in range(2):
            u = 2 * rp + lo
            score_sum[u] = (score[0, u] + score[1, u]) + (score[2, u] + score[3, u])
            for i in range(2):
                small(score_sum.at[u], score_in.at[ex], lo * Z + 2 * rp + i, s_send, s_recv)

    named = dict(Z=stage_z, Y=stage_y, C=compute, A=add_x, F=finish, G=give)
    stages = [(named[n], LAGS[n]) for n in SEQ]

    def step(k, carry):
        @pl.when(k < PAIRS - AHEAD)
        def _():
            send_z(k + AHEAD)

        @pl.when(k == LAGS["F"] - 1)
        def _():
            take_prob()

        for stage, lag in stages:

            @pl.when(jnp.logical_and(k >= lag, k < PAIRS + lag))
            def _(stage=stage, lag=lag):
                stage(k - lag)

        return carry

    lax.fori_loop(0, PAIRS + max(LAGS.values()), step, 0)

    for i in range(0, SLOTS, 128):
        for j in range(0, FP, 128):
            out_buf[j : j + 128, i : i + 128] = jnp.transpose(result[i : i + 128, j : j + 128]).astype(BF16)
    store = pltpu.make_async_copy(out_buf.at[pl.ds(0, FFX)], gh_hbm.at[0], local_sem.at[3])
    store.start()

    pltpu.make_async_copy(score_in, score_in, s_recv).wait()
    for e in range(EXP):
        table[e : e + 1, :] = score_in[e]
    by_lane = jnp.transpose(table[...])[:, 0:EXP]
    for k in range(2):
        spread = dot(by_lane, hot[k], precision=lax.Precision.HIGHEST)
        mine = iota((TOK, TOK), 0) == slots[k, 0:1, :]
        gp_ref[k : k + 1, :] = jnp.sum(jnp.where(mine, spread, 0.0), axis=0, keepdims=True)

    small_sent(prob_in, p_send)
    small_sent(score_in, s_send)
    sent = send.at[pl.ds(0, Z - 1)]
    pltpu.make_async_copy(sent, sent, z_send).wait()
    for i in range(3):
        pltpu.make_async_copy(other, other, y_send.at[i]).wait()
    for ys in range(4):
        pltpu.make_async_copy(other, other, sib_send.at[ys]).wait()
    for i in range(3):
        pltpu.make_async_copy(relay, relay, xs_send.at[i]).wait()
    three = score.at[pl.ds(0, 3)]
    pltpu.make_async_copy(three, three, dp_send).wait()
    store.wait()


def shards(grad_out, routes, probs, hidden, weight):
    dma = pltpu.SemaphoreType.DMA
    vmem, hbm = pl.BlockSpec(memory_space=pltpu.VMEM), pl.BlockSpec(memory_space=pl.ANY)
    grad_hidden, grad_probs = pl.pallas_call(
        kernel,
        out_shape=(
            jax.ShapeDtypeStruct((1, FFX, SLOTS), BF16),
            jax.ShapeDtypeStruct((2, TOK), F32),
        ),
        in_specs=[hbm, vmem, vmem, hbm, hbm],
        out_specs=(hbm, vmem),
        scratch_shapes=[
            pltpu.VMEM((TOK, D), BF16),
            pltpu.VMEM((Z, 16, MSG), BF16),
            pltpu.VMEM((Z, 16, MSG), BF16),
            pltpu.VMEM((PAIRS, 16, MSG), BF16),
            pltpu.VMEM((2, 4, PAIRS, 16, MSG), BF16),
            pltpu.VMEM((FP, D), BF16),
            pltpu.VMEM((FP, SLOTS), BF16),
            pltpu.VMEM((SLOTS, FP), F32),
            pltpu.VMEM((UNITS, 4, 24, FP), F32),
            pltpu.VMEM((UNITS, 24, FP), F32),
            pltpu.VMEM((2, UNITS, 24, FP), F32),
            pltpu.VMEM((SLOTS, FP), F32),
            pltpu.VMEM((FP, SLOTS), BF16),
            pltpu.VMEM((EXP, 1, TOK), F32),
            pltpu.VMEM((EXP, 1, TOK), F32),
            pltpu.VMEM((SLOTS, TOK), F32),
            pltpu.VMEM((4, UNITS, 1, TOK), F32),
            pltpu.VMEM((UNITS, 1, TOK), F32),
            pltpu.VMEM((EXP, 1, TOK), F32),
            pltpu.VMEM((TOK, TOK), F32),
            pltpu.VMEM((2, EXP, TOK), F32),
            pltpu.VMEM((2, 8, TOK), jnp.int32),
            dma((4,)),
            dma,
            dma((Z,)),
            dma((3,)),
            dma((4,)),
            dma((2, 4, PAIRS)),
            dma,
            dma,
            dma((3,)),
            dma((UNITS,)),
            dma((2, UNITS)),
            dma,
            dma((PAIRS,)),
            dma,
            dma,
        ],
        compiler_params=pltpu.CompilerParams(
            collective_id=0, has_side_effects=True, vmem_limit_bytes=60 * 1024 * 1024
        ),
        name="moe_down_backward",
    )(grad_out, routes.T, probs.T, jnp.swapaxes(hidden, 1, 2), weight)
    return jnp.swapaxes(grad_hidden, 1, 2), grad_probs.T


def solution(mesh):
    return jax.shard_map(
        shards,
        mesh=mesh,
        in_specs=(
            P(("dp", "expert"), "tensor"),
            P(("dp", "expert"), None),
            P(("dp", "expert"), None),
            P("expert", "tensor", "dp"),
            P("expert", "dp", "tensor"),
        ),
        out_specs=(P("expert", "tensor", "dp"), P(("dp", "expert"), None)),
        check_vma=False,
    )
```

```python
import jax
import jax.numpy as jnp
from jax import lax
from jax.experimental import pallas as pl
from jax.experimental.pallas import tpu as pltpu
from jax.sharding import PartitionSpec as P

ORDER = (0, 1, -1, 3, -3, 4, 2, -2)
MESH = pl.DeviceIdType.MESH
F32 = jnp.float32
BF16 = jnp.bfloat16

TOK = 128
CAP = 12
Z = 16
PAIRS = Z // 2
EXP = 2 * Z
D = 1792
HALF = D // 2
MSG = D + HALF
FFX = 608
FP = 640
SLOTS = 384
UNITS = 2 * PAIRS


def iota(shape, dim):
    return lax.broadcasted_iota(jnp.int32, shape, dim)


def dot(a, b, **kw):
    return jnp.dot(a, b, preferred_element_type=F32, **kw)


def dot_t(a, b):
    return lax.dot_general(a, b, (((1,), (1,)), ((), ())), preferred_element_type=F32)


def offset(k):
    at = ORDER[0]
    for i, o in enumerate(ORDER[1:], 1):
        at = jnp.where(k == i, o, at)
    return at


def turn(lo):
    return 1 if lo == 0 else 3


def kernel(
    grad_hbm, routes_ref, probs_ref, hidden_hbm, weight_hbm,
    gh_hbm, gp_ref,
    tokens, send, zbuf, other, recv, w_buf, h_buf, natural, hidden, part, relay, fin, result, out_buf,
    prob_out, prob_mid, prob_in, prob_col, score, group_in, score_sum, score_in, table, hot, slots,
    local_sem, h_send, h_recv, z_send, z_recv, y_send, sib_send, x_recv,
    p_send, p_recv, q_send, q_recv, xs_send, relay_recv, fin_recv, g_send, g_recv, s_send, s_recv,
):
    dp = lax.axis_index("dp")
    ex = lax.axis_index("expert")
    x = lax.axis_index("tensor")
    h, c = lax.div(dp, 2), lax.rem(dp, 2)
    l, z = lax.div(ex, Z), lax.rem(ex, Z)
    y = 2 * h + l
    pair = lax.div(z, 2)
    group = 4 * dp + x
    sibling = (2 * h + 1 - c, ex, x)
    opposite = (2 * (1 - h) + c, ex, x)
    beside = ((c, (1 - l) * Z + z, x), (2 + c, (1 - l) * Z + z, x))

    load_grad = pltpu.make_async_copy(grad_hbm, tokens, local_sem.at[0])
    load_w = pltpu.make_async_copy(weight_hbm.at[0], w_buf.at[pl.ds(0, FFX)], local_sem.at[1])
    load_h = pltpu.make_async_copy(hidden_hbm.at[0], h_buf.at[x, pl.ds(0, FFX)], local_sem.at[2])
    load_grad.start()
    load_w.start()
    load_h.start()

    barrier = pltpu.get_barrier_semaphore()

    def greet(device):
        pl.semaphore_signal(barrier, inc=1, device_id=device, device_id_type=MESH)

    def greet_line(i, carry):
        greet((dp, lax.rem(ex + i, EXP), x))
        return carry

    def greet_group(i, carry):
        g = lax.rem(group + i, 16)
        greet((lax.div(g, 4), ex, lax.rem(g, 4)))
        return carry

    lax.fori_loop(1, EXP, greet_line, 0)
    lax.fori_loop(1, 16, greet_group, 0)
    greet((2 * (1 - h) + c, (1 - l) * Z + z, x))

    expert = iota((EXP, TOK), 0)
    hots = [(routes_ref[k : k + 1, :] == expert).astype(F32) for k in range(2)]
    both = hots[0] + hots[1]
    before = (iota((TOK, TOK), 0) < iota((TOK, TOK), 1)).astype(BF16)
    earlier = dot(both.astype(BF16), before)
    number = jnp.where(both > 0, earlier + 1.0, 0.0).astype(BF16)
    row, col = iota((SLOTS, EXP), 0), iota((SLOTS, EXP), 1)
    first, rest = row < 16 * Z, row - 16 * Z
    zz = jnp.where(first, row >> 4, rest >> 3)
    lam = jnp.where(first, (row >> 3) & 1, (rest >> 2) & 1)
    spread = dot((col == lam * Z + zz).astype(BF16), number)
    row = iota((SLOTS, TOK), 0)
    slot = jnp.where(row < 16 * Z, row & 7, 8 + (row & 3))
    select = (spread == (slot + 1).astype(F32)).astype(BF16)

    load_grad.wait()
    for n in range(0, D, 256):
        block = dot(select[0 : 16 * Z], tokens[:, n : n + 256])
        send[:, :, n : n + 256] = block.reshape(Z, 16, 256).astype(BF16)
    for n in range(0, HALF, 128):
        halves = []
        for at in (n, HALF + n):
            block = dot(select[16 * Z :], tokens[:, at : at + 128])
            halves.append(block.reshape(Z, 8, 128))
        send[:, :, D + n : D + n + 128] = jnp.concatenate(halves, axis=1).astype(BF16)

    def small(source, target, n, sent, got):
        @pl.when(n == ex)
        def _():
            pltpu.make_async_copy(source, target, got).start()

        @pl.when(n != ex)
        def _():
            pltpu.make_async_remote_copy(
                source, target, sent, got, device_id=(dp, n, x), device_id_type=MESH
            ).start()

    probs = probs_ref[...].astype(F32)
    weights = jnp.zeros((EXP, TOK), F32)
    zz = lax.rem(z, 2)
    for k in range(2):
        at = jnp.sum(hots[k] * earlier, axis=0, keepdims=True).astype(jnp.int32)
        weights += dot_t(
            (hots[k] * probs[k : k + 1, :]).astype(BF16), (iota((TOK, TOK), 0) == at).astype(BF16)
        )
        hot[k] = hots[k]
        slots[k] = jnp.broadcast_to(jnp.where(at < 8, 8 * zz + at, 8 + 4 * zz + at), (8, TOK))
    for e in range(EXP):
        prob_out[e] = weights[e : e + 1, :]
    load_h.wait()

    pl.semaphore_wait(barrier, 47)

    def send_prob(n, carry):
        small(prob_out.at[n], prob_mid.at[ex], n, p_send, p_recv)
        return carry

    lax.fori_loop(0, EXP, send_prob, 0)

    def send_z(i, carry):
        to = 2 * lax.rem(pair + offset(lax.div(i, 2)) + PAIRS, PAIRS) + lax.rem(i, 2)

        @pl.when(to == z)
        def _():
            pltpu.make_async_copy(send.at[to], zbuf.at[z], z_recv.at[z]).start()

        @pl.when(to != z)
        def _():
            pltpu.make_async_remote_copy(
                send.at[to], zbuf.at[z], z_send, z_recv.at[z],
                device_id=(dp, l * Z + to, x), device_id_type=MESH,
            ).start()

        return carry

    lax.fori_loop(0, Z, send_z, 0)

    own_hidden = h_buf.at[x, pl.ds(0, FFX)]
    for i in range(1, 4):
        pltpu.make_async_remote_copy(
            own_hidden, own_hidden, h_send, h_recv.at[x],
            device_id=(dp, ex, lax.rem(x + i, 4)), device_id_type=MESH,
        ).start()
    w_buf[FFX:FP, :] = jnp.zeros((FP - FFX, D), BF16)
    for i in range(4):
        h_buf[i, FFX:FP, :] = jnp.zeros((FP - FFX, SLOTS), BF16)
    table[...] = jnp.zeros((TOK, TOK), F32)
    load_w.wait()

    def take_hidden(xs, carry):
        @pl.when(xs != x)
        def _():
            ref = h_buf.at[xs, pl.ds(0, FFX)]
            pltpu.make_async_copy(ref, ref, h_recv.at[xs]).wait()

        for i in range(0, SLOTS, 128):
            for j in range(0, FP, 128):
                natural[i : i + 128, j : j + 128] = jnp.transpose(
                    h_buf[xs, j : j + 128, i : i + 128].astype(F32)
                )

        def permute(u, inner):
            rows = pl.multiple_of(24 * u, 8)
            low = iota((8, FP), 0) < 4
            a, b = natural[pl.ds(rows + 8, 8), :], natural[pl.ds(rows + 16, 8), :]
            hidden[xs, pl.ds(rows, 8), :] = natural[pl.ds(rows, 8), :]
            hidden[xs, pl.ds(rows + 8, 8), :] = jnp.where(low, pltpu.roll(a, 4, 0), pltpu.roll(b, 4, 0))
            hidden[xs, pl.ds(rows + 16, 8), :] = jnp.where(low, a, b)
            return inner

        return lax.fori_loop(0, UNITS, permute, carry)

    def pass_prob():
        pltpu.make_async_copy(prob_mid, prob_mid, p_recv).wait()

        @pl.when(x == dp)
        def _():
            pltpu.make_async_copy(prob_mid, prob_in, q_recv).start()

        @pl.when(x != dp)
        def _():
            pltpu.make_async_remote_copy(
                prob_mid, prob_in, q_send, q_recv, device_id=(x, ex, dp), device_id_type=MESH
            ).start()

    def take_prob():
        pltpu.make_async_copy(prob_in, prob_in, q_recv).wait()
        for e in range(EXP):
            table[e : e + 1, :] = prob_in[e]
        row, col = iota((SLOTS, EXP), 0), iota((SLOTS, EXP), 1)
        spread = dot(((row * 5462) >> 16 == col).astype(BF16), table[0:EXP].astype(BF16))
        row, col = iota((SLOTS, TOK), 0), iota((SLOTS, TOK), 1)
        mine = row - CAP * ((row * 5462) >> 16) == col
        prob_col[...] = jnp.broadcast_to(
            jnp.sum(jnp.where(mine, spread, 0.0), axis=1, keepdims=True), (SLOTS, TOK)
        )

    def origin(k):
        return lax.rem(pair - offset(k) + PAIRS, PAIRS)

    def forward(source, core, ys, rp, sent, device):
        pltpu.make_async_remote_copy(
            source, recv.at[core, ys, rp], sent, x_recv.at[core, ys, rp], device_id=device, device_id_type=MESH
        ).start()

    def arrived(core, ys, rp):
        ref = recv.at[core, ys, rp]
        pltpu.make_async_copy(ref, ref, x_recv.at[core, ys, rp]).wait()

    def stage_z(k):
        rp = origin(k)
        for i in range(2):
            ref = zbuf.at[2 * rp + i]
            pltpu.make_async_copy(ref, ref, z_recv.at[2 * rp + i]).wait()
        both = zbuf[pl.ds(2 * rp, 2)].reshape(32, MSG)
        row, col = iota((32, 32), 0), iota((32, 32), 1)
        v = jnp.where(row < 16, l, 1 - l)
        eight, four = row & 7, row & 3
        whole = dot((col == 16 * ((row >> 3) & 1) + 8 * v + eight).astype(BF16), both[:, :D]).astype(BF16)
        at = 16 * ((eight >> 2) & 1) + 8 * ((row >> 3) & 1) + 4 * v + four
        folded = dot((col == at).astype(BF16), both[:, D:]).astype(BF16)
        recv[c, y, rp, :, 0:D] = whole[0:16]
        recv[c, y, rp, :, D:MSG] = folded[0:16]
        other[rp, :, 0:D] = whole[16:32]
        other[rp, :, D:MSG] = folded[16:32]
        forward(other.at[rp], c, y, rp, y_send.at[0], beside[0])
        forward(other.at[rp], c, y, rp, y_send.at[1], beside[1])
        forward(recv.at[c, y, rp], c, y, rp, y_send.at[2], opposite)
        forward(recv.at[c, y, rp], c, y, rp, sib_send.at[y], sibling)

    def stage_y(k):
        rp = origin(k)
        for i in (1, 3, 2):
            ys = lax.rem(y + i, 4)
            arrived(c, ys, rp)
            forward(recv.at[c, ys, rp], c, ys, rp, sib_send.at[ys], sibling)

    def along_x(i, source, target, got, device_x):
        pltpu.make_async_remote_copy(
            source, target, xs_send.at[i], got, device_id=(dp, ex, device_x), device_id_type=MESH
        ).start()

    def compute(k):
        rp = origin(k)
        for ys in range(4):
            arrived(1 - c, ys, rp)
        rows = [(lo, hi, core) for lo in range(2) for hi in range(2) for core in range(2)]
        whole = [recv[core, 2 * hi + lo, rp, :, 0:D] for lo, hi, core in rows]
        folded = [recv[core, 2 * hi + lo, rp, :, D:MSG] for lo, hi, core in rows]
        left_rows = jnp.concatenate([v[:, :HALF] for v in whole] + folded, axis=0)
        right_rows = jnp.concatenate([v[:, HALF:] for v in whole] + folded, axis=0)
        for n0, n1 in ((0, 256), (256, 512), (512, 640)):
            left = dot_t(left_rows, w_buf[n0:n1, :HALF])
            right = dot_t(right_rows, w_buf[n0:n1, HALF:])
            for i, (lo, hi, core) in enumerate(rows):
                at = 16 * i
                part[2 * rp + lo, 2 * hi + core, 0:16, n0:n1] = left[at : at + 16] + right[at : at + 16]
                at += 128
                part[2 * rp + lo, 2 * hi + core, 16:24, n0:n1] = left[at : at + 8] + right[at + 8 : at + 16]
        for lo in range(2):
            u, s = 2 * rp + lo, turn(lo)
            along_x(0, part.at[u, lax.rem(x + 2, 4)], relay.at[u], relay_recv.at[u], lax.rem(x + s, 4))
            back_x = lax.rem(x + 4 - s, 4)
            along_x(1, part.at[u, back_x], fin.at[1, u], fin_recv.at[1, u], back_x)

    def add_x(k):
        rp = origin(k)
        for lo in range(2):
            u = 2 * rp + lo
            to = lax.rem(x + turn(lo), 4)
            pltpu.make_async_copy(relay.at[u], relay.at[u], relay_recv.at[u]).wait()
            relay[u] = part[u, to] + relay[u]
            along_x(2, relay.at[u], fin.at[0, u], fin_recv.at[0, u], to)

    def finish(k):
        rp = origin(k)
        for lo in range(2):
            u = 2 * rp + lo
            for i in range(2):
                pltpu.make_async_copy(fin.at[i, u], fin.at[i, u], fin_recv.at[i, u]).wait()
            total = part[u, x] + (fin[0, u] + fin[1, u])
            low = iota((8, FP), 0) < 4
            middle, end = pltpu.roll(total[8:16], 4, 0), total[16:24]
            total = jnp.concatenate(
                [total[0:8], jnp.where(low, end, middle), jnp.where(low, middle, end)], axis=0
            )
            rows = pl.ds(pl.multiple_of(192 * lo + 24 * rp, 8), 24)
            result[rows, :] = prob_col[rows, 0:1] * total

    def scores(k):
        rp = origin(k)
        for lo in range(2):
            u = 2 * rp + lo
            rows = pl.ds(pl.multiple_of(192 * lo + 24 * rp, 8), 24)
            for d in range(4):
                col = jnp.sum(hidden[d, rows, :] * part[u, d], axis=1, keepdims=True)
                score[d, u] = jnp.sum(
                    jnp.where(iota((24, TOK), 0) == iota((24, TOK), 1), col, 0.0), axis=0, keepdims=True
                )
            group_in[group, u] = score[dp, u]

        def exchange(i, carry):
            g = lax.rem(group + i, 16)
            to = lax.div(g, 4)
            pltpu.make_async_remote_copy(
                score.at[to, pl.ds(2 * rp, 2)], group_in.at[group, pl.ds(2 * rp, 2)], g_send, g_recv.at[rp],
                device_id=(to, ex, lax.rem(g, 4)), device_id_type=MESH,
            ).start()
            return carry

        lax.fori_loop(1, 16, exchange, 0)

    def give(k):
        rp = origin(k)
        others = group_in.at[pl.ds(0, 15), pl.ds(0, 2)]
        pltpu.make_async_copy(others, others, g_recv.at[rp]).wait()
        for lo in range(2):
            u = 2 * rp + lo
            rows = [group_in[g, u] for g in range(16)]
            while len(rows) > 1:
                rows = [a + b for a, b in zip(rows[::2], rows[1::2], strict=True)]
            score_sum[u] = rows[0]
            for i in range(2):
                small(score_sum.at[u], score_in.at[ex], lo * Z + 2 * rp + i, s_send, s_recv)

    def step(k, carry):
        def at(first, last, stage, *args):
            @pl.when(jnp.logical_and(k >= first, k <= last))
            def _():
                stage(*args)

        last = PAIRS - 1
        at(1, 1, pass_prob)
        at(2, 2, take_prob)
        at(3, 3, lambda: lax.fori_loop(0, 4, take_hidden, 0))
        at(0, last, stage_z, k)
        at(1, last + 1, stage_y, k - 1)
        at(1, last + 1, compute, k - 1)
        at(3, 3, scores, k - 3)
        at(3, 3, scores, k - 2)
        at(3, last + 1, scores, k - 1)
        at(4, 4, give, k - 4)
        at(4, 4, give, k - 3)
        at(4, last + 2, give, k - 2)
        at(2, last + 2, add_x, k - 2)
        at(3, last + 3, finish, k - 3)
        return carry

    lax.fori_loop(0, PAIRS + 3, step, 0)

    for i in range(0, SLOTS, 128):
        for j in range(0, FP, 128):
            out_buf[j : j + 128, i : i + 128] = jnp.transpose(result[i : i + 128, j : j + 128]).astype(BF16)
    store = pltpu.make_async_copy(out_buf.at[pl.ds(0, FFX)], gh_hbm.at[0], local_sem.at[3])
    store.start()

    pltpu.make_async_copy(score_in, score_in, s_recv).wait()
    for e in range(EXP):
        table[e : e + 1, :] = score_in[e]
    by_lane = jnp.transpose(table[...])[:, 0:EXP]
    for k in range(2):
        spread = dot(by_lane, hot[k], precision=lax.Precision.HIGHEST)
        mine = iota((TOK, TOK), 0) == slots[k, 0:1, :]
        gp_ref[k : k + 1, :] = jnp.sum(jnp.where(mine, spread, 0.0), axis=0, keepdims=True)

    for ref, sem in ((prob_mid, p_send), (score_in, s_send)):
        ref = ref.at[pl.ds(0, EXP - 1)]
        pltpu.make_async_copy(ref, ref, sem).wait()

    @pl.when(x != dp)
    def _():
        pltpu.make_async_copy(prob_mid, prob_mid, q_send).wait()

    ref = h_buf.at[pl.ds(0, 3), pl.ds(0, FFX)]
    pltpu.make_async_copy(ref, ref, h_send).wait()
    sent = send.at[pl.ds(0, Z - 1)]
    pltpu.make_async_copy(sent, sent, z_send).wait()
    for i in range(3):
        pltpu.make_async_copy(other, other, y_send.at[i]).wait()
    for ys in range(4):
        pltpu.make_async_copy(other, other, sib_send.at[ys]).wait()
    for i in range(3):
        pltpu.make_async_copy(relay, relay, xs_send.at[i]).wait()
    others = group_in.at[pl.ds(0, 15)]
    pltpu.make_async_copy(others, others, g_send).wait()
    store.wait()


def shards(grad_out, routes, probs, hidden, weight):
    dma = pltpu.SemaphoreType.DMA
    vmem, hbm = pl.BlockSpec(memory_space=pltpu.VMEM), pl.BlockSpec(memory_space=pl.ANY)
    grad_hidden, grad_probs = pl.pallas_call(
        kernel,
        out_shape=(
            jax.ShapeDtypeStruct((1, FFX, SLOTS), BF16),
            jax.ShapeDtypeStruct((2, TOK), F32),
        ),
        in_specs=[hbm, vmem, vmem, hbm, hbm],
        out_specs=(hbm, vmem),
        scratch_shapes=[
            pltpu.VMEM((TOK, D), BF16),
            pltpu.VMEM((Z, 16, MSG), BF16),
            pltpu.VMEM((Z, 16, MSG), BF16),
            pltpu.VMEM((PAIRS, 16, MSG), BF16),
            pltpu.VMEM((2, 4, PAIRS, 16, MSG), BF16),
            pltpu.VMEM((FP, D), BF16),
            pltpu.VMEM((4, FP, SLOTS), BF16),
            pltpu.VMEM((SLOTS, FP), F32),
            pltpu.VMEM((4, SLOTS, FP), F32),
            pltpu.VMEM((UNITS, 4, 24, FP), F32),
            pltpu.VMEM((UNITS, 24, FP), F32),
            pltpu.VMEM((2, UNITS, 24, FP), F32),
            pltpu.VMEM((SLOTS, FP), F32),
            pltpu.VMEM((FP, SLOTS), BF16),
            pltpu.VMEM((EXP, 1, TOK), F32),
            pltpu.VMEM((EXP, 1, TOK), F32),
            pltpu.VMEM((EXP, 1, TOK), F32),
            pltpu.VMEM((SLOTS, TOK), F32),
            pltpu.VMEM((4, UNITS, 1, TOK), F32),
            pltpu.VMEM((16, UNITS, 1, TOK), F32),
            pltpu.VMEM((UNITS, 1, TOK), F32),
            pltpu.VMEM((EXP, 1, TOK), F32),
            pltpu.VMEM((TOK, TOK), F32),
            pltpu.VMEM((2, EXP, TOK), F32),
            pltpu.VMEM((2, 8, TOK), jnp.int32),
            dma((4,)),
            dma,
            dma((4,)),
            dma,
            dma((Z,)),
            dma((3,)),
            dma((4,)),
            dma((2, 4, PAIRS)),
            dma,
            dma,
            dma,
            dma,
            dma((3,)),
            dma((UNITS,)),
            dma((2, UNITS)),
            dma,
            dma((PAIRS,)),
            dma,
            dma,
        ],
        compiler_params=pltpu.CompilerParams(
            collective_id=0, has_side_effects=True, vmem_limit_bytes=60 * 1024 * 1024
        ),
        name="moe_down_backward",
    )(grad_out, routes.T, probs.T, jnp.swapaxes(hidden, 1, 2), weight)
    return jnp.swapaxes(grad_hidden, 1, 2), grad_probs.T


def solution(mesh):
    return jax.shard_map(
        shards,
        mesh=mesh,
        in_specs=(
            P(("dp", "expert"), "tensor"),
            P(("dp", "expert"), None),
            P(("dp", "expert"), None),
            P("expert", "tensor", "dp"),
            P("expert", "dp", "tensor"),
        ),
        out_specs=(P("expert", "tensor", "dp"), P(("dp", "expert"), None)),
        check_vma=False,
    )
```

```python
import jax
import jax.numpy as jnp
from jax import lax
from jax.experimental import pallas as pl
from jax.experimental.pallas import tpu as pltpu
from jax.sharding import PartitionSpec as P

ORDER = (0, 1, -1, 3, -3, 2, 4, -2)
MESH = pl.DeviceIdType.MESH
F32 = jnp.float32
BF16 = jnp.bfloat16

TOK = 128
CAP = 12
Z = 16
PAIRS = Z // 2
EXP = 2 * Z
D = 1792
HALF = D // 2
MSG = D + HALF
FFX = 608
FP = 640
SLOTS = 384
UNITS = 2 * PAIRS


def iota(shape, dim):
    return lax.broadcasted_iota(jnp.int32, shape, dim)


def dot(a, b, **kw):
    return jnp.dot(a, b, preferred_element_type=F32, **kw)


def dot_t(a, b):
    return lax.dot_general(a, b, (((1,), (1,)), ((), ())), preferred_element_type=F32)


def offset(k):
    at = ORDER[0]
    for i, o in enumerate(ORDER[1:], 1):
        at = jnp.where(k == i, o, at)
    return at


def turn(lo):
    return 1 if lo == 0 else 3


def kernel(
    grad_hbm, routes_ref, probs_ref, hidden_hbm, weight_hbm,
    gh_hbm, gp_ref,
    tokens, send, zbuf, other, recv, w_buf, h_buf, natural, hidden, part, relay, fin, result, out_buf,
    prob_out, prob_mid, prob_in, prob_col, score, group_in, score_sum, score_in, table, hot, slots,
    local_sem, h_send, h_recv, z_send, z_recv, y_send, sib_send, x_recv,
    p_send, p_recv, q_send, q_recv, xs_send, relay_recv, fin_recv, g_send, g_recv, s_send, s_recv,
):
    dp = lax.axis_index("dp")
    ex = lax.axis_index("expert")
    x = lax.axis_index("tensor")
    h, c = lax.div(dp, 2), lax.rem(dp, 2)
    l, z = lax.div(ex, Z), lax.rem(ex, Z)
    y = 2 * h + l
    pair = lax.div(z, 2)
    group = 4 * dp + x
    sibling = (2 * h + 1 - c, ex, x)
    opposite = (2 * (1 - h) + c, ex, x)
    beside = ((c, (1 - l) * Z + z, x), (2 + c, (1 - l) * Z + z, x))

    load_grad = pltpu.make_async_copy(grad_hbm, tokens, local_sem.at[0])
    load_w = pltpu.make_async_copy(weight_hbm.at[0], w_buf.at[pl.ds(0, FFX)], local_sem.at[1])
    load_h = pltpu.make_async_copy(hidden_hbm.at[0], h_buf.at[x, pl.ds(0, FFX)], local_sem.at[2])
    load_grad.start()
    load_w.start()
    load_h.start()

    barrier = pltpu.get_barrier_semaphore()

    def greet(device):
        pl.semaphore_signal(barrier, inc=1, device_id=device, device_id_type=MESH)

    def greet_line(i, carry):
        greet((dp, lax.rem(ex + i, EXP), x))
        return carry

    def greet_group(i, carry):
        g = lax.rem(group + i, 16)
        greet((lax.div(g, 4), ex, lax.rem(g, 4)))
        return carry

    lax.fori_loop(1, EXP, greet_line, 0)
    lax.fori_loop(1, 16, greet_group, 0)
    greet((2 * (1 - h) + c, (1 - l) * Z + z, x))

    expert = iota((EXP, TOK), 0)
    hots = [(routes_ref[k : k + 1, :] == expert).astype(F32) for k in range(2)]
    both = hots[0] + hots[1]
    before = (iota((TOK, TOK), 0) < iota((TOK, TOK), 1)).astype(BF16)
    earlier = dot(both.astype(BF16), before)
    number = jnp.where(both > 0, earlier + 1.0, 0.0).astype(BF16)
    row, col = iota((SLOTS, EXP), 0), iota((SLOTS, EXP), 1)
    first, rest = row < 16 * Z, row - 16 * Z
    zz = jnp.where(first, row >> 4, rest >> 3)
    lam = jnp.where(first, (row >> 3) & 1, (rest >> 2) & 1)
    spread = dot((col == lam * Z + zz).astype(BF16), number)
    row = iota((SLOTS, TOK), 0)
    slot = jnp.where(row < 16 * Z, row & 7, 8 + (row & 3))
    select = (spread == (slot + 1).astype(F32)).astype(BF16)

    load_grad.wait()
    for n in range(0, D, 256):
        block = dot(select[0 : 16 * Z], tokens[:, n : n + 256])
        send[:, :, n : n + 256] = block.reshape(Z, 16, 256).astype(BF16)
    for n in range(0, HALF, 128):
        halves = []
        for at in (n, HALF + n):
            block = dot(select[16 * Z :], tokens[:, at : at + 128])
            halves.append(block.reshape(Z, 8, 128))
        send[:, :, D + n : D + n + 128] = jnp.concatenate(halves, axis=1).astype(BF16)

    def small(source, target, n, sent, got):
        @pl.when(n == ex)
        def _():
            pltpu.make_async_copy(source, target, got).start()

        @pl.when(n != ex)
        def _():
            pltpu.make_async_remote_copy(
                source, target, sent, got, device_id=(dp, n, x), device_id_type=MESH
            ).start()

    probs = probs_ref[...].astype(F32)
    weights = jnp.zeros((EXP, TOK), F32)
    zz = lax.rem(z, 2)
    for k in range(2):
        at = jnp.sum(hots[k] * earlier, axis=0, keepdims=True).astype(jnp.int32)
        weights += dot_t(
            (hots[k] * probs[k : k + 1, :]).astype(BF16), (iota((TOK, TOK), 0) == at).astype(BF16)
        )
        hot[k] = hots[k]
        slots[k] = jnp.broadcast_to(jnp.where(at < 8, 8 * zz + at, 8 + 4 * zz + at), (8, TOK))
    for e in range(EXP):
        prob_out[e] = weights[e : e + 1, :]
    load_h.wait()

    pl.semaphore_wait(barrier, 47)

    def send_prob(n, carry):
        small(prob_out.at[n], prob_mid.at[ex], n, p_send, p_recv)
        return carry

    lax.fori_loop(0, EXP, send_prob, 0)

    def send_z(i, carry):
        to = 2 * lax.rem(pair + offset(lax.div(i, 2)) + PAIRS, PAIRS) + lax.rem(i, 2)

        @pl.when(to == z)
        def _():
            pltpu.make_async_copy(send.at[to], zbuf.at[z], z_recv.at[z]).start()

        @pl.when(to != z)
        def _():
            pltpu.make_async_remote_copy(
                send.at[to], zbuf.at[z], z_send, z_recv.at[z],
                device_id=(dp, l * Z + to, x), device_id_type=MESH,
            ).start()

        return carry

    lax.fori_loop(0, Z, send_z, 0)

    own_hidden = h_buf.at[x, pl.ds(0, FFX)]
    for i in range(1, 4):
        pltpu.make_async_remote_copy(
            own_hidden, own_hidden, h_send, h_recv.at[x],
            device_id=(dp, ex, lax.rem(x + i, 4)), device_id_type=MESH,
        ).start()
    w_buf[FFX:FP, :] = jnp.zeros((FP - FFX, D), BF16)
    for i in range(4):
        h_buf[i, FFX:FP, :] = jnp.zeros((FP - FFX, SLOTS), BF16)
    table[...] = jnp.zeros((TOK, TOK), F32)
    load_w.wait()

    def take_hidden(xs, carry):
        @pl.when(xs != x)
        def _():
            ref = h_buf.at[xs, pl.ds(0, FFX)]
            pltpu.make_async_copy(ref, ref, h_recv.at[xs]).wait()

        for i in range(0, SLOTS, 128):
            for j in range(0, FP, 128):
                natural[i : i + 128, j : j + 128] = jnp.transpose(
                    h_buf[xs, j : j + 128, i : i + 128].astype(F32)
                )

        def permute(u, inner):
            rows = pl.multiple_of(24 * u, 8)
            low = iota((8, FP), 0) < 4
            a, b = natural[pl.ds(rows + 8, 8), :], natural[pl.ds(rows + 16, 8), :]
            hidden[xs, pl.ds(rows, 8), :] = natural[pl.ds(rows, 8), :]
            hidden[xs, pl.ds(rows + 8, 8), :] = jnp.where(low, pltpu.roll(a, 4, 0), pltpu.roll(b, 4, 0))
            hidden[xs, pl.ds(rows + 16, 8), :] = jnp.where(low, a, b)
            return inner

        return lax.fori_loop(0, UNITS, permute, carry)

    def pass_prob():
        pltpu.make_async_copy(prob_mid, prob_mid, p_recv).wait()

        @pl.when(x == dp)
        def _():
            pltpu.make_async_copy(prob_mid, prob_in, q_recv).start()

        @pl.when(x != dp)
        def _():
            pltpu.make_async_remote_copy(
                prob_mid, prob_in, q_send, q_recv, device_id=(x, ex, dp), device_id_type=MESH
            ).start()

    def take_prob():
        pltpu.make_async_copy(prob_in, prob_in, q_recv).wait()
        for e in range(EXP):
            table[e : e + 1, :] = prob_in[e]
        row, col = iota((SLOTS, EXP), 0), iota((SLOTS, EXP), 1)
        spread = dot(((row * 5462) >> 16 == col).astype(BF16), table[0:EXP].astype(BF16))
        row, col = iota((SLOTS, TOK), 0), iota((SLOTS, TOK), 1)
        mine = row - CAP * ((row * 5462) >> 16) == col
        prob_col[...] = jnp.broadcast_to(
            jnp.sum(jnp.where(mine, spread, 0.0), axis=1, keepdims=True), (SLOTS, TOK)
        )

    def origin(k):
        return lax.rem(pair - offset(k) + PAIRS, PAIRS)

    def forward(source, core, ys, rp, sent, device):
        pltpu.make_async_remote_copy(
            source, recv.at[core, ys, rp], sent, x_recv.at[core, ys, rp], device_id=device, device_id_type=MESH
        ).start()

    def arrived(core, ys, rp):
        ref = recv.at[core, ys, rp]
        pltpu.make_async_copy(ref, ref, x_recv.at[core, ys, rp]).wait()

    def stage_z(k):
        rp = origin(k)
        for i in range(2):
            ref = zbuf.at[2 * rp + i]
            pltpu.make_async_copy(ref, ref, z_recv.at[2 * rp + i]).wait()
        both = zbuf[pl.ds(2 * rp, 2)].reshape(32, MSG)
        row, col = iota((32, 32), 0), iota((32, 32), 1)
        v = jnp.where(row < 16, l, 1 - l)
        eight, four = row & 7, row & 3
        whole = dot((col == 16 * ((row >> 3) & 1) + 8 * v + eight).astype(BF16), both[:, :D]).astype(BF16)
        at = 16 * ((eight >> 2) & 1) + 8 * ((row >> 3) & 1) + 4 * v + four
        folded = dot((col == at).astype(BF16), both[:, D:]).astype(BF16)
        recv[c, y, rp, :, 0:D] = whole[0:16]
        recv[c, y, rp, :, D:MSG] = folded[0:16]
        other[rp, :, 0:D] = whole[16:32]
        other[rp, :, D:MSG] = folded[16:32]
        forward(other.at[rp], c, y, rp, y_send.at[0], beside[0])
        forward(other.at[rp], c, y, rp, y_send.at[1], beside[1])
        forward(recv.at[c, y, rp], c, y, rp, y_send.at[2], opposite)
        forward(recv.at[c, y, rp], c, y, rp, sib_send.at[y], sibling)

    def stage_y(k):
        rp = origin(k)
        for i in (1, 3, 2):
            ys = lax.rem(y + i, 4)
            arrived(c, ys, rp)
            forward(recv.at[c, ys, rp], c, ys, rp, sib_send.at[ys], sibling)

    def along_x(i, source, target, got, device_x):
        pltpu.make_async_remote_copy(
            source, target, xs_send.at[i], got, device_id=(dp, ex, device_x), device_id_type=MESH
        ).start()

    def compute(k):
        rp = origin(k)
        for ys in range(4):
            arrived(1 - c, ys, rp)
        rows = [(lo, hi, core) for lo in range(2) for hi in range(2) for core in range(2)]
        whole = [recv[core, 2 * hi + lo, rp, :, 0:D] for lo, hi, core in rows]
        folded = [recv[core, 2 * hi + lo, rp, :, D:MSG] for lo, hi, core in rows]
        left_rows = jnp.concatenate([v[:, :HALF] for v in whole] + folded, axis=0)
        right_rows = jnp.concatenate([v[:, HALF:] for v in whole] + folded, axis=0)
        for n0, n1 in ((0, 256), (256, 512), (512, 640)):
            left = dot_t(left_rows, w_buf[n0:n1, :HALF])
            right = dot_t(right_rows, w_buf[n0:n1, HALF:])
            for i, (lo, hi, core) in enumerate(rows):
                at = 16 * i
                part[2 * rp + lo, 2 * hi + core, 0:16, n0:n1] = left[at : at + 16] + right[at : at + 16]
                at += 128
                part[2 * rp + lo, 2 * hi + core, 16:24, n0:n1] = left[at : at + 8] + right[at + 8 : at + 16]
        for lo in range(2):
            u, s = 2 * rp + lo, turn(lo)
            along_x(0, part.at[u, lax.rem(x + 2, 4)], relay.at[u], relay_recv.at[u], lax.rem(x + s, 4))
            back_x = lax.rem(x + 4 - s, 4)
            along_x(1, part.at[u, back_x], fin.at[1, u], fin_recv.at[1, u], back_x)

    def add_x(k):
        rp = origin(k)
        for lo in range(2):
            u = 2 * rp + lo
            to = lax.rem(x + turn(lo), 4)
            pltpu.make_async_copy(relay.at[u], relay.at[u], relay_recv.at[u]).wait()
            relay[u] = part[u, to] + relay[u]
            along_x(2, relay.at[u], fin.at[0, u], fin_recv.at[0, u], to)

    def finish(k):
        rp = origin(k)
        for lo in range(2):
            u = 2 * rp + lo
            for i in range(2):
                pltpu.make_async_copy(fin.at[i, u], fin.at[i, u], fin_recv.at[i, u]).wait()
            total = part[u, x] + (fin[0, u] + fin[1, u])
            low = iota((8, FP), 0) < 4
            middle, end = pltpu.roll(total[8:16], 4, 0), total[16:24]
            total = jnp.concatenate(
                [total[0:8], jnp.where(low, end, middle), jnp.where(low, middle, end)], axis=0
            )
            rows = pl.ds(pl.multiple_of(192 * lo + 24 * rp, 8), 24)
            result[rows, :] = prob_col[rows, 0:1] * total

    def scores(k):
        rp = origin(k)
        for lo in range(2):
            u = 2 * rp + lo
            rows = pl.ds(pl.multiple_of(192 * lo + 24 * rp, 8), 24)
            for d in range(4):
                col = jnp.sum(hidden[d, rows, :] * part[u, d], axis=1, keepdims=True)
                score[d, u] = jnp.sum(
                    jnp.where(iota((24, TOK), 0) == iota((24, TOK), 1), col, 0.0), axis=0, keepdims=True
                )
            group_in[group, u] = score[dp, u]

        def exchange(i, carry):
            g = lax.rem(group + i, 16)
            to = lax.div(g, 4)
            pltpu.make_async_remote_copy(
                score.at[to, pl.ds(2 * rp, 2)], group_in.at[group, pl.ds(2 * rp, 2)], g_send, g_recv.at[rp],
                device_id=(to, ex, lax.rem(g, 4)), device_id_type=MESH,
            ).start()
            return carry

        lax.fori_loop(1, 16, exchange, 0)

    def give(k):
        rp = origin(k)
        others = group_in.at[pl.ds(0, 15), pl.ds(0, 2)]
        pltpu.make_async_copy(others, others, g_recv.at[rp]).wait()
        for lo in range(2):
            u = 2 * rp + lo
            rows = [group_in[g, u] for g in range(16)]
            while len(rows) > 1:
                rows = [a + b for a, b in zip(rows[::2], rows[1::2], strict=True)]
            score_sum[u] = rows[0]
            for i in range(2):
                small(score_sum.at[u], score_in.at[ex], lo * Z + 2 * rp + i, s_send, s_recv)

    def step(k, carry):
        def at(first, last, stage, *args):
            @pl.when(jnp.logical_and(k >= first, k <= last))
            def _():
                stage(*args)

        last = PAIRS - 1
        at(1, 1, pass_prob)
        at(2, 2, take_prob)
        at(3, 3, lambda: lax.fori_loop(0, 4, take_hidden, 0))
        at(0, last, stage_z, k)
        at(1, last + 1, stage_y, k - 1)
        at(1, last + 1, compute, k - 1)
        at(3, 3, scores, k - 3)
        at(3, 3, scores, k - 2)
        at(3, last + 1, scores, k - 1)
        at(4, 4, give, k - 4)
        at(4, 4, give, k - 3)
        at(4, last + 2, give, k - 2)
        at(2, last + 2, add_x, k - 2)
        at(3, last + 3, finish, k - 3)
        return carry

    lax.fori_loop(0, PAIRS + 3, step, 0)

    for i in range(0, SLOTS, 128):
        for j in range(0, FP, 128):
            out_buf[j : j + 128, i : i + 128] = jnp.transpose(result[i : i + 128, j : j + 128]).astype(BF16)
    store = pltpu.make_async_copy(out_buf.at[pl.ds(0, FFX)], gh_hbm.at[0], local_sem.at[3])
    store.start()

    pltpu.make_async_copy(score_in, score_in, s_recv).wait()
    for e in range(EXP):
        table[e : e + 1, :] = score_in[e]
    by_lane = jnp.transpose(table[...])[:, 0:EXP]
    for k in range(2):
        spread = dot(by_lane, hot[k], precision=lax.Precision.HIGHEST)
        mine = iota((TOK, TOK), 0) == slots[k, 0:1, :]
        gp_ref[k : k + 1, :] = jnp.sum(jnp.where(mine, spread, 0.0), axis=0, keepdims=True)

    for ref, sem in ((prob_mid, p_send), (score_in, s_send)):
        ref = ref.at[pl.ds(0, EXP - 1)]
        pltpu.make_async_copy(ref, ref, sem).wait()

    @pl.when(x != dp)
    def _():
        pltpu.make_async_copy(prob_mid, prob_mid, q_send).wait()

    ref = h_buf.at[pl.ds(0, 3), pl.ds(0, FFX)]
    pltpu.make_async_copy(ref, ref, h_send).wait()
    sent = send.at[pl.ds(0, Z - 1)]
    pltpu.make_async_copy(sent, sent, z_send).wait()
    for i in range(3):
        pltpu.make_async_copy(other, other, y_send.at[i]).wait()
    for ys in range(4):
        pltpu.make_async_copy(other, other, sib_send.at[ys]).wait()
    for i in range(3):
        pltpu.make_async_copy(relay, relay, xs_send.at[i]).wait()
    others = group_in.at[pl.ds(0, 15)]
    pltpu.make_async_copy(others, others, g_send).wait()
    store.wait()


def shards(grad_out, routes, probs, hidden, weight):
    dma = pltpu.SemaphoreType.DMA
    vmem, hbm = pl.BlockSpec(memory_space=pltpu.VMEM), pl.BlockSpec(memory_space=pl.ANY)
    grad_hidden, grad_probs = pl.pallas_call(
        kernel,
        out_shape=(
            jax.ShapeDtypeStruct((1, FFX, SLOTS), BF16),
            jax.ShapeDtypeStruct((2, TOK), F32),
        ),
        in_specs=[hbm, vmem, vmem, hbm, hbm],
        out_specs=(hbm, vmem),
        scratch_shapes=[
            pltpu.VMEM((TOK, D), BF16),
            pltpu.VMEM((Z, 16, MSG), BF16),
            pltpu.VMEM((Z, 16, MSG), BF16),
            pltpu.VMEM((PAIRS, 16, MSG), BF16),
            pltpu.VMEM((2, 4, PAIRS, 16, MSG), BF16),
            pltpu.VMEM((FP, D), BF16),
            pltpu.VMEM((4, FP, SLOTS), BF16),
            pltpu.VMEM((SLOTS, FP), F32),
            pltpu.VMEM((4, SLOTS, FP), F32),
            pltpu.VMEM((UNITS, 4, 24, FP), F32),
            pltpu.VMEM((UNITS, 24, FP), F32),
            pltpu.VMEM((2, UNITS, 24, FP), F32),
            pltpu.VMEM((SLOTS, FP), F32),
            pltpu.VMEM((FP, SLOTS), BF16),
            pltpu.VMEM((EXP, 1, TOK), F32),
            pltpu.VMEM((EXP, 1, TOK), F32),
            pltpu.VMEM((EXP, 1, TOK), F32),
            pltpu.VMEM((SLOTS, TOK), F32),
            pltpu.VMEM((4, UNITS, 1, TOK), F32),
            pltpu.VMEM((16, UNITS, 1, TOK), F32),
            pltpu.VMEM((UNITS, 1, TOK), F32),
            pltpu.VMEM((EXP, 1, TOK), F32),
            pltpu.VMEM((TOK, TOK), F32),
            pltpu.VMEM((2, EXP, TOK), F32),
            pltpu.VMEM((2, 8, TOK), jnp.int32),
            dma((4,)),
            dma,
            dma((4,)),
            dma,
            dma((Z,)),
            dma((3,)),
            dma((4,)),
            dma((2, 4, PAIRS)),
            dma,
            dma,
            dma,
            dma,
            dma((3,)),
            dma((UNITS,)),
            dma((2, UNITS)),
            dma,
            dma((PAIRS,)),
            dma,
            dma,
        ],
        compiler_params=pltpu.CompilerParams(
            collective_id=0, has_side_effects=True, vmem_limit_bytes=60 * 1024 * 1024
        ),
        name="moe_down_backward",
    )(grad_out, routes.T, probs.T, jnp.swapaxes(hidden, 1, 2), weight)
    return jnp.swapaxes(grad_hidden, 1, 2), grad_probs.T


def solution(mesh):
    return jax.shard_map(
        shards,
        mesh=mesh,
        in_specs=(
            P(("dp", "expert"), "tensor"),
            P(("dp", "expert"), None),
            P(("dp", "expert"), None),
            P("expert", "tensor", "dp"),
            P("expert", "dp", "tensor"),
        ),
        out_specs=(P("expert", "tensor", "dp"), P(("dp", "expert"), None)),
        check_vma=False,
    )
```
